32 devices in a mesh: groups: 1, row: 8 (over z, y), col: 4 (over x, core).
Axes of the slice: x: 2, y: 2, z: 4, core: 2. Of those that a mesh axis runs over, the one named last changes fastest.
Arguments:
- activations: bfloat16 [1024, 16384], P('groups', ('row', 'col')), may hold values from -2.5 to 2.5
- token_ids: int32 [1024], P('groups'), may hold values from 0 to 128255
- initial: float32 [16384, 256], P(('groups', 'row', 'col')), may hold values from -6 to 6
- block_mask: int32 [128, 2], P('groups'), may hold values 0 or 1
Outputs:
- gram: float32 [8, 4, 512, 16384], P('groups', 'col', None, 'row')
- repaired: float32 [16384, 256], P(('groups', 'row', 'col'))
The draws below stay inside these ranges and needn't reach their ends.
All inputs are finite; a program needn't handle non-finite values.
Results may differ from the reference program's by a relative error of at most 0.0003.
Values may be sent and summed in bfloat16 or wider, within the bound.
A program may use at most 128 MiB of HBM per device.

```python
import math
import jax
import jax.numpy as jnp
import numpy as np
from jax import lax

D = 16384
VOCAB = 128256
ROWS = 1024
OUTC = 256
BLOCK = 128
ITERS = 2
SHARD = 512
N_ROW = 8
N_COL = 4


def draw_activations(key, part):
    entry_key = jax.random.fold_in(key, 11)
    values = jnp.clip(jax.random.normal(entry_key, (ROWS, D), jnp.float32), -2.5, 2.5)
    return values.astype(jnp.bfloat16)


def set_ends(result, rng, least, top_value):
    spot = [jax.random.randint(jax.random.fold_in(rng, axis), (), 0, length) for axis, length in enumerate(result.shape)]
    longest = result.shape.index(max(result.shape))
    next_to = spot[:longest] + [(spot[longest] + 1) % result.shape[longest]] + spot[longest + 1:]
    return result.at[tuple(spot)].set(least).at[tuple(next_to)].set(top_value)


def levels(key, extent, split, smallest, high):
    gain, own = 1.0, jax.random.fold_in(key, 6)
    for dim, blocks in split:
        steps = jnp.exp(jax.random.uniform(jax.random.fold_in(own, dim), (blocks,), jnp.float32, smallest / len(split), high / len(split)))
        gain = gain * jnp.repeat(steps, extent[dim] // blocks).reshape([-1 if axis == dim else 1 for axis in range(len(extent))])
    return gain


def skewed_wide(rng, shape, count, slope):
    loads = [min(1 << octave, count + 1 - (1 << octave)) * (1 << 20) // math.isqrt((1 << octave) ** slope) + 1 for octave in range((count + 1).bit_length()) if 1 << octave <= count]
    deviation = 1 + sum(loads) // (1 << 30)
    listing = np.cumsum(np.array([max(1, weight // deviation) for weight in loads]))
    ticket = jax.random.randint(jax.random.fold_in(rng, 1), shape, 0, int(listing[len(loads) - 1]))
    start = jnp.left_shift(1, jnp.searchsorted(jnp.asarray(listing, jnp.int32), ticket, side="right").astype(jnp.int32))
    standing = start - 1 + jax.random.randint(jax.random.fold_in(rng, 4), shape, 0, 1 << 30) % jnp.minimum(start, count + 1 - start)
    return jax.random.permutation(jax.random.fold_in(rng, 2), count)[standing].astype(jnp.int32)


def noise(own_key, dims, spread, most, split=(), held_as=jnp.bfloat16):
    drawn = jax.random.normal(own_key, dims, jnp.float32) * spread
    if len(split) > 0:
        drawn = levels(own_key, dims, split, -0.22, 0.18) * drawn
    return jnp.clip(drawn, min=-most, max=most).astype(held_as)


def setup_inputs(seed: int = 0, part: int = 0) -> dict:
    splits = jax.random.split(jax.random.key(seed), 5)
    part_splits = jax.random.split(jax.random.fold_in(splits[4], part), 5)
    activations = draw_activations(jax.random.fold_in(jax.random.fold_in(splits[4], part), 71), part)
    token_ids = set_ends(skewed_wide(part_splits[1], (ROWS,), VOCAB, 2), jax.random.fold_in(part_splits[1], 3), 0, VOCAB - 1).astype(jnp.int32)
    initial = noise(part_splits[2], (D, OUTC), 1.0, 6.0, ((0, 32),), jnp.float32)
    block_mask = set_ends((jax.random.randint(part_splits[3], (D // BLOCK, OUTC // BLOCK), 0, 2) < 1).astype(jnp.int32), jax.random.fold_in(part_splits[3], 1), 0, 1)
    return dict(activations=activations, token_ids=token_ids, initial=initial, block_mask=block_mask)


def reference(activations, token_ids, initial, block_mask):
    matches = (token_ids[:, None] == token_ids[None, :]).astype(jnp.float32)
    weights = 1.0 / lax.optimization_barrier(jnp.sum(matches, axis=1))
    weighted = (activations.astype(jnp.float32) * weights[:, None]).astype(jnp.bfloat16)
    gram_full = lax.dot_general(weighted.astype(jnp.float32), activations.astype(jnp.float32), (((0,), (0,)), ((), ())), precision=lax.Precision.HIGHEST) * (1.0 / ROWS)
    mask_full = jnp.repeat(jnp.repeat(block_mask.astype(jnp.float32), BLOCK, axis=0), BLOCK, axis=1)
    step_size = ROWS / (D + 2.0 * math.sqrt(D * ROWS) + ROWS)
    current = mask_full * initial
    for iteration in range(ITERS):
        change_now = current - initial
        pulled = jnp.dot(gram_full, change_now, precision=lax.Precision.HIGHEST)
        current = mask_full * (current - step_size * pulled)
    return (gram_full.reshape(N_ROW, N_COL, SHARD, D), current)
```

```python
import functools
import math

import jax
import jax.numpy as jnp
from jax import lax
from jax.experimental import pallas as pl
from jax.experimental.pallas import tpu as pltpu
from jax.sharding import PartitionSpec as P

BLOCK = 128
ITERS = 2
PIECES = 2
VMEM_LIMIT = 48 * 1024 * 1024


def split_two(value):
    high = value.astype(jnp.bfloat16)
    return high, (value - high.astype(jnp.float32)).astype(jnp.bfloat16)


def exchange_kernel(
    n_row, n_col, step_size,
    wt_hbm, act_hbm, wt, act, init, mask,
    wt_all, act_all, cur,
    partial, from_col, part, from_row, tot, change2, tot2,
    gs, gr, xs, xr, own_sem, s1, r1, s2, r2, s3, r3, s4, r4,
):
    rows = act.shape[0]
    feats, outc = init.shape
    r, c = lax.axis_index("row"), lax.axis_index("col")
    z, y = r // 2, r % 2
    nz = n_row // 2
    x, core = c // 2, c % 2
    nx = n_col // 2
    up, down, side = r + 2, r - 2, z * 2 + (1 - y)
    sibling = x * 2 + (1 - core)
    row_peers = [lax.rem(r + k, n_row) for k in range(1, n_row)]
    col_peers = [lax.rem(c + k, n_col) for k in range(1, n_col)]

    barrier = pltpu.get_barrier_semaphore()
    for p in row_peers:
        pl.semaphore_signal(barrier, inc=1, device_id={"row": p}, device_id_type=pl.DeviceIdType.MESH)
    for p in col_peers:
        pl.semaphore_signal(barrier, inc=1, device_id={"col": p}, device_id_type=pl.DeviceIdType.MESH)
    pl.semaphore_wait(barrier, n_row + n_col - 2)

    def send(src, dst, ss, rs, where):
        return pltpu.make_async_remote_copy(
            src_ref=src, dst_ref=dst, send_sem=ss, recv_sem=rs,
            device_id=where, device_id_type=pl.DeviceIdType.MESH)

    def gcopy(a, h, way, peer, own=False):
        src = wt_hbm.at[h] if own else wt_all.at[a, h]
        return send(src, wt_all.at[a, h], gs.at[way, a, h], gr.at[a, h], {"row": peer})

    def own_pieces(act_on):
        for h in range(PIECES):
            @pl.when(z + 1 < nz)
            def _():
                act_on(gcopy(r, h, 0, up, True))

            @pl.when(z > 0)
            def _():
                act_on(gcopy(r, h, 1, down, True))

            act_on(gcopy(r, h, 2, side, True))

    def hop(d, h, act_on, arrive):
        @pl.when(z >= d)
        def _():
            a = r - 2 * d
            if arrive:
                gcopy(a, h, 2, side).wait_recv()

            @pl.when(z + 1 < nz)
            def _():
                act_on(gcopy(a, h, 0, up))

            act_on(gcopy(a, h, 2, side))

        @pl.when(z + d < nz)
        def _():
            a = r + 2 * d
            if arrive:
                gcopy(a, h, 2, side).wait_recv()

            @pl.when(z > 0)
            def _():
                act_on(gcopy(a, h, 1, down))

            act_on(gcopy(a, h, 2, side))

    start = lambda copy: copy.start()
    wait_send = lambda copy: copy.wait_send()

    hops = [(d, h) for d in range(1, nz) for h in range(PIECES)]
    hops_done = [0]

    def next_hop():
        if hops_done[0] < len(hops):
            d, h = hops[hops_done[0]]
            hop(d, h, start, True)
            hops_done[0] += 1

    def x_copies():
        copies = []
        for k in range(1, nx):
            p = lax.rem(x + k, nx) * 2 + core
            copies.append(send(act_hbm, act_all.at[c], xs.at[k], xr.at[c], {"col": p}))
        copies.append(send(act_hbm, act_all.at[c], xs.at[0], xr.at[c], {"col": sibling}))
        return copies

    def x_passed(k):
        a = lax.rem(x + k, nx) * 2 + core
        return send(act_all.at[a], act_all.at[a], xs.at[nx + k], xr.at[a], {"col": sibling})

    own_wt = pltpu.make_async_copy(wt_hbm, wt_all.at[r], own_sem.at[0])
    own_act = pltpu.make_async_copy(act_hbm, act_all.at[c], own_sem.at[1])
    own_pieces(start)

    chunk = rows // n_col
    cur[...] = mask[...] * init[...]
    pending = []

    for it in range(ITERS):
        high, low = split_two(cur[...] - init[...])
        change2[:, 0:outc] = high
        change2[:, outc:2 * outc] = low

        def project(j, carry):
            a = act[pl.ds(pl.multiple_of(j * chunk, chunk), chunk), :]
            both = jnp.dot(a, change2[...], preferred_element_type=jnp.float32)
            total = both[:, 0:outc] + both[:, outc:2 * outc]
            partial[it, j] = total.reshape(partial.shape[2:])
            return carry

        lax.fori_loop(0, n_col, project, 0)

        def exchange(copies):
            for copy in copies:
                copy.start()
            pending.extend(copies)

        exchange([send(partial.at[it, p], from_col.at[it, c], s1.at[it, k], r1.at[it, c], {"col": p})
                  for k, p in enumerate(col_peers)])
        if it == 0:
            own_wt.start()
            own_act.start()
        next_hop()
        for k, p in enumerate(col_peers):
            send(partial.at[it, p], from_col.at[it, p], s1.at[it, k], r1.at[it, p], {"col": p}).wait_recv()
        acc = partial[it, c]
        for p in col_peers:
            acc = acc + from_col[it, p]
        part[it] = acc
        exchange([send(part.at[it, p], from_row.at[it, r], s2.at[it, k], r2.at[it, r], {"row": p})
                  for k, p in enumerate(row_peers)])
        if it == 0:
            for copy in x_copies():
                copy.start()
        next_hop()
        for k, p in enumerate(row_peers):
            send(part.at[it, p], from_row.at[it, p], s2.at[it, k], r2.at[it, p], {"row": p}).wait_recv()
        acc = part[it, r]
        for p in row_peers:
            acc = acc + from_row[it, p]
        tot[it, c, r] = acc
        exchange([send(tot.at[it, c, r], tot.at[it, c, r], s3.at[it, k], r3.at[it, r], {"row": p})
                  for k, p in enumerate(row_peers)])
        if it > 0:
            next_hop()
        for k, p in enumerate(row_peers):
            send(tot.at[it, c, p], tot.at[it, c, p], s3.at[it, k], r3.at[it, p], {"row": p}).wait_recv()
        exchange([send(tot.at[it, c], tot.at[it, c], s4.at[it, k], r4.at[it, c], {"col": p})
                  for k, p in enumerate(col_peers)])
        next_hop()
        if it == 0:
            for k in range(1, nx):
                a = lax.rem(x + k, nx) * 2 + core
                x_passed(k).wait_recv()
                x_passed(k).start()
        for k, p in enumerate(col_peers):
            send(tot.at[it, p], tot.at[it, p], s4.at[it, k], r4.at[it, p], {"col": p}).wait_recv()

        high, low = split_two(tot[it].reshape(rows, outc))
        tot2[:, 0:outc] = high
        tot2[:, outc:2 * outc] = low

        def pull(j, carry):
            at = pl.ds(pl.multiple_of(j * BLOCK, BLOCK), BLOCK)
            both = jnp.dot(wt[at, :], tot2[...], preferred_element_type=jnp.float32)
            pulled = (both[:, 0:outc] + both[:, outc:2 * outc]) * (1.0 / rows)
            cur[at, :] = mask[at, :] * (cur[at, :] - step_size * pulled)
            return carry

        lax.fori_loop(0, feats // BLOCK, pull, 0)

    while hops_done[0] < len(hops):
        next_hop()
    for zz in range(nz):
        for h in range(PIECES):
            gcopy(zz * 2 + (1 - y), h, 2, side).wait_recv()
    for k in range(nx):
        a = lax.rem(x + k, nx) * 2 + (1 - core)
        send(act_all.at[a], act_all.at[a], xs.at[0], xr.at[a], {"col": sibling}).wait_recv()
    own_pieces(wait_send)
    for d, h in hops:
        hop(d, h, wait_send, False)
    for copy in x_copies():
        copy.wait_send()
    for k in range(1, nx):
        x_passed(k).wait_send()
    for copy in pending:
        copy.wait_send()
    own_wt.wait()
    own_act.wait()


def gram_kernel(scale, wt, act, out):
    feats = act.shape[2]
    for j in range(act.shape[0]):
        tile = jnp.dot(wt[0], act[j], preferred_element_type=jnp.float32) * scale
        out[0, 0, :, j * feats:(j + 1) * feats] = tile


def expanded_mask(block_mask, shard_rows, col_count):
    first_feature = (lax.axis_index("row") * col_count + lax.axis_index("col")) * shard_rows
    block_index = (first_feature + jnp.arange(shard_rows, dtype=jnp.int32)) // BLOCK
    selector = (
        block_index[:, None] == jnp.arange(block_mask.shape[0], dtype=jnp.int32)[None, :]
    ).astype(jnp.float32)
    mask_rows = jnp.dot(selector, block_mask.astype(jnp.float32), precision=lax.Precision.HIGHEST)
    return jnp.repeat(mask_rows, BLOCK, axis=1)


def weigh(activations, token_ids):
    matches = (token_ids[:, None] == token_ids[None, :]).astype(jnp.float32)
    weights = 1.0 / jnp.sum(matches, axis=1)
    return (activations.astype(jnp.float32) * weights[:, None]).astype(jnp.bfloat16)


def kernel_shards(n_row, n_col, activations, token_ids, initial, block_mask):
    rows, feats = activations.shape
    outc = initial.shape[1]
    depth = feats * n_row * n_col
    step_size = rows / (depth + 2.0 * math.sqrt(depth * rows) + rows)
    wt = weigh(activations, token_ids).T
    mask = expanded_mask(block_mask, feats, n_col)
    bf, f32 = jnp.bfloat16, jnp.float32
    small = rows // (n_row * n_col)
    dma = pltpu.SemaphoreType.DMA
    nx = n_col // 2
    any_spec = pl.BlockSpec(memory_space=pl.ANY)
    vmem_spec = pl.BlockSpec(memory_space=pltpu.VMEM)
    wt_cut = wt.reshape(PIECES, feats // PIECES, rows)
    wt_all, act_all, current = pl.pallas_call(
        functools.partial(exchange_kernel, n_row, n_col, step_size),
        out_shape=(
            jax.ShapeDtypeStruct((n_row, PIECES, feats // PIECES, rows), bf),
            jax.ShapeDtypeStruct((n_col, rows, feats), bf),
            jax.ShapeDtypeStruct((feats, outc), f32),
        ),
        in_specs=[any_spec, any_spec] + [vmem_spec] * 4,
        out_specs=(any_spec, any_spec, vmem_spec),
        scratch_shapes=[
            pltpu.VMEM((ITERS, n_col, n_row, small, outc), f32),
            pltpu.VMEM((ITERS, n_col, n_row, small, outc), f32),
            pltpu.VMEM((ITERS, n_row, small, outc), f32),
            pltpu.VMEM((ITERS, n_row, small, outc), f32),
            pltpu.VMEM((ITERS, n_col, n_row, small, outc), f32),
            pltpu.VMEM((feats, 2 * outc), bf),
            pltpu.VMEM((rows, 2 * outc), bf),
            dma((3, n_row, PIECES)), dma((n_row, PIECES)),
            dma((2 * nx,)), dma((n_col,)), dma((2,)),
            dma((ITERS, n_col)), dma((ITERS, n_col)),
            dma((ITERS, n_row)), dma((ITERS, n_row)),
            dma((ITERS, n_row)), dma((ITERS, n_row)),
            dma((ITERS, n_col)), dma((ITERS, n_col)),
        ],
        compiler_params=pltpu.CompilerParams(
            collective_id=0, has_side_effects=True, vmem_limit_bytes=VMEM_LIMIT),
    )(wt_cut, activations, wt, activations, initial, mask)

    tile = feats // PIECES
    wt_tiles = wt_all.reshape(n_row * PIECES, tile, rows)
    gram = pl.pallas_call(
        functools.partial(gram_kernel, 1.0 / rows),
        grid=(n_row * PIECES,),
        out_shape=jax.ShapeDtypeStruct((n_row, 1, feats, n_col * feats), f32),
        in_specs=[
            pl.BlockSpec((1, tile, rows), lambda i: (i, 0, 0)),
            pl.BlockSpec((n_col, rows, feats), lambda i: (0, 0, 0)),
        ],
        out_specs=pl.BlockSpec((1, 1, tile, n_col * feats), lambda i: (i // PIECES, 0, i % PIECES, 0)),
        compiler_params=pltpu.CompilerParams(vmem_limit_bytes=VMEM_LIMIT),
    )(wt_tiles, act_all)
    return gram, current


def shards(n_row, n_col, activations, token_ids, initial, block_mask):
    rows, feats = activations.shape
    if feats % (BLOCK * PIECES) == 0 and n_row % 2 == 0 and n_col % 2 == 0 and rows % (8 * n_row * n_col) == 0:
        return kernel_shards(n_row, n_col, activations, token_ids, initial, block_mask)
    weighted = weigh(activations, token_ids)
    column_panel = lax.all_gather(activations, "col", axis=1, tiled=True)
    gram_tile = lax.dot_general(
        lax.all_gather(weighted, "row", axis=1, tiled=True),
        column_panel,
        (((0,), (0,)), ((), ())),
        preferred_element_type=jnp.float32,
    ) * (1.0 / rows)
    mask_full = expanded_mask(block_mask, feats, n_col)
    depth = feats * n_row * n_col
    step_size = rows / (depth + 2.0 * math.sqrt(depth * rows) + rows)
    current = mask_full * initial
    for iteration in range(ITERS):
        change_now = current - initial
        projected = jnp.dot(
            activations.astype(jnp.float32), change_now, precision=lax.Precision.HIGHEST
        )
        totals = lax.psum(projected, ("row", "col"))
        pulled = lax.dot_general(
            weighted.astype(jnp.float32),
            totals,
            (((0,), (0,)), ((), ())),
            precision=lax.Precision.HIGHEST,
        ) * (1.0 / rows)
        current = mask_full * (current - step_size * pulled)
    return gram_tile.reshape(n_row, 1, feats, gram_tile.shape[1]), current


def solution(mesh):
    in_specs = (
        P("groups", ("row", "col")),
        P("groups"),
        P(("groups", "row", "col"), None),
        P("groups", None),
    )
    out_specs = (P("groups", "col", None, "row"), P(("groups", "row", "col"), None))
    body = functools.partial(shards, mesh.shape["row"], mesh.shape["col"])
    return jax.shard_map(body, mesh=mesh, in_specs=in_specs, out_specs=out_specs, check_vma=False)
```

```python
import functools
import math

import jax
import jax.numpy as jnp
from jax import lax
from jax.experimental import pallas as pl
from jax.experimental.pallas import tpu as pltpu
from jax.sharding import PartitionSpec as P

BLOCK = 128
ITERS = 2
PIECES = 2
VMEM_LIMIT = 48 * 1024 * 1024


def split_two(value):
    high = value.astype(jnp.bfloat16)
    return high, (value - high.astype(jnp.float32)).astype(jnp.bfloat16)


def exchange_kernel(
    n_row, n_col, step_size,
    wt_hbm, act_hbm, wt, act, init, mask,
    wt_all, act_all, cur,
    partial, from_col, part, from_row, tot, change2, tot2,
    gs, gr, xs, xr, own_sem, s1, r1, s2, r2, s3, r3, s4, r4,
):
    rows = act.shape[0]
    feats, outc = init.shape
    r, c = lax.axis_index("row"), lax.axis_index("col")
    z, y = r // 2, r % 2
    nz = n_row // 2
    x, core = c // 2, c % 2
    nx = n_col // 2
    up, down, side = r + 2, r - 2, z * 2 + (1 - y)
    sibling = x * 2 + (1 - core)
    row_peers = [lax.rem(r + k, n_row) for k in range(1, n_row)]
    col_peers = [lax.rem(c + k, n_col) for k in range(1, n_col)]

    barrier = pltpu.get_barrier_semaphore()
    for p in row_peers:
        pl.semaphore_signal(barrier, inc=1, device_id={"row": p}, device_id_type=pl.DeviceIdType.MESH)
    for p in col_peers:
        pl.semaphore_signal(barrier, inc=1, device_id={"col": p}, device_id_type=pl.DeviceIdType.MESH)
    pl.semaphore_wait(barrier, n_row + n_col - 2)

    def send(src, dst, ss, rs, where):
        return pltpu.make_async_remote_copy(
            src_ref=src, dst_ref=dst, send_sem=ss, recv_sem=rs,
            device_id=where, device_id_type=pl.DeviceIdType.MESH)

    def gcopy(a, h, way, peer, own=False):
        src = wt_hbm.at[h] if own else wt_all.at[a, h]
        return send(src, wt_all.at[a, h], gs.at[way, a, h], gr.at[a, h], {"row": peer})

    def own_pieces(act_on):
        for h in range(PIECES):
            @pl.when(z + 1 < nz)
            def _():
                act_on(gcopy(r, h, 0, up, True))

            @pl.when(z > 0)
            def _():
                act_on(gcopy(r, h, 1, down, True))

            act_on(gcopy(r, h, 2, side, True))

    def hop(d, h, act_on, arrive):
        @pl.when(z >= d)
        def _():
            a = r - 2 * d
            if arrive:
                gcopy(a, h, 2, side).wait_recv()

            @pl.when(z + 1 < nz)
            def _():
                act_on(gcopy(a, h, 0, up))

            act_on(gcopy(a, h, 2, side))

        @pl.when(z + d < nz)
        def _():
            a = r + 2 * d
            if arrive:
                gcopy(a, h, 2, side).wait_recv()

            @pl.when(z > 0)
            def _():
                act_on(gcopy(a, h, 1, down))

            act_on(gcopy(a, h, 2, side))

    start = lambda copy: copy.start()
    wait_send = lambda copy: copy.wait_send()

    hops = [(d, h) for d in range(1, nz) for h in range(PIECES)]
    hops_done = [0]

    def next_hop():
        if hops_done[0] < len(hops):
            d, h = hops[hops_done[0]]
            hop(d, h, start, True)
            hops_done[0] += 1

    def x_copies():
        copies = []
        for k in range(1, nx):
            p = lax.rem(x + k, nx) * 2 + core
            copies.append(send(act_hbm, act_all.at[c], xs.at[k], xr.at[c], {"col": p}))
        copies.append(send(act_hbm, act_all.at[c], xs.at[0], xr.at[c], {"col": sibling}))
        return copies

    def x_passed(k):
        a = lax.rem(x + k, nx) * 2 + core
        return send(act_all.at[a], act_all.at[a], xs.at[nx + k], xr.at[a], {"col": sibling})

    own_wt = pltpu.make_async_copy(wt_hbm, wt_all.at[r], own_sem.at[0])
    own_act = pltpu.make_async_copy(act_hbm, act_all.at[c], own_sem.at[1])
    own_pieces(start)

    chunk = rows // n_col
    cur[...] = mask[...] * init[...]
    pending = []

    for it in range(ITERS):
        high, low = split_two(cur[...] - init[...])
        change2[:, 0:outc] = high
        change2[:, outc:2 * outc] = low

        def project(j, carry):
            a = act[pl.ds(pl.multiple_of(j * chunk, chunk), chunk), :]
            both = jnp.dot(a, change2[...], preferred_element_type=jnp.float32)
            total = both[:, 0:outc] + both[:, outc:2 * outc]
            partial[it, j] = total.reshape(partial.shape[2:])
            return carry

        lax.fori_loop(0, n_col, project, 0)

        def exchange(copies):
            for copy in copies:
                copy.start()
            pending.extend(copies)

        exchange([send(partial.at[it, p], from_col.at[it, c], s1.at[it, k], r1.at[it, c], {"col": p})
                  for k, p in enumerate(col_peers)])
        if it == 0:
            own_wt.start()
            own_act.start()
        next_hop()
        for k, p in enumerate(col_peers):
            send(partial.at[it, p], from_col.at[it, p], s1.at[it, k], r1.at[it, p], {"col": p}).wait_recv()
        acc = partial[it, c]
        for p in col_peers:
            acc = acc + from_col[it, p]
        part[it] = acc
        exchange([send(part.at[it, p], from_row.at[it, r], s2.at[it, k], r2.at[it, r], {"row": p})
                  for k, p in enumerate(row_peers)])
        if it == 0:
            for copy in x_copies():
                copy.start()
        next_hop()
        for k, p in enumerate(row_peers):
            send(part.at[it, p], from_row.at[it, p], s2.at[it, k], r2.at[it, p], {"row": p}).wait_recv()
        acc = part[it, r]
        for p in row_peers:
            acc = acc + from_row[it, p]
        tot[it, c, r] = acc
        exchange([send(tot.at[it, c, r], tot.at[it, c, r], s3.at[it, k], r3.at[it, r], {"row": p})
                  for k, p in enumerate(row_peers)])
        next_hop()
        for k, p in enumerate(row_peers):
            send(tot.at[it, c, p], tot.at[it, c, p], s3.at[it, k], r3.at[it, p], {"row": p}).wait_recv()
        exchange([send(tot.at[it, c], tot.at[it, c], s4.at[it, k], r4.at[it, c], {"col": p})
                  for k, p in enumerate(col_peers)])
        next_hop()
        if it == 0:
            for k in range(1, nx):
                a = lax.rem(x + k, nx) * 2 + core
                x_passed(k).wait_recv()
                x_passed(k).start()
        for k, p in enumerate(col_peers):
            send(tot.at[it, p], tot.at[it, p], s4.at[it, k], r4.at[it, p], {"col": p}).wait_recv()

        high, low = split_two(tot[it].reshape(rows, outc))
        tot2[:, 0:outc] = high
        tot2[:, outc:2 * outc] = low

        def pull(j, carry):
            at = pl.ds(pl.multiple_of(j * BLOCK, BLOCK), BLOCK)
            both = jnp.dot(wt[at, :], tot2[...], preferred_element_type=jnp.float32)
            pulled = (both[:, 0:outc] + both[:, outc:2 * outc]) * (1.0 / rows)
            cur[at, :] = mask[at, :] * (cur[at, :] - step_size * pulled)
            return carry

        lax.fori_loop(0, feats // BLOCK, pull, 0)

    while hops_done[0] < len(hops):
        next_hop()
    for zz in range(nz):
        for h in range(PIECES):
            gcopy(zz * 2 + (1 - y), h, 2, side).wait_recv()
    for k in range(nx):
        a = lax.rem(x + k, nx) * 2 + (1 - core)
        send(act_all.at[a], act_all.at[a], xs.at[0], xr.at[a], {"col": sibling}).wait_recv()
    own_pieces(wait_send)
    for d, h in hops:
        hop(d, h, wait_send, False)
    for copy in x_copies():
        copy.wait_send()
    for k in range(1, nx):
        x_passed(k).wait_send()
    for copy in pending:
        copy.wait_send()
    own_wt.wait()
    own_act.wait()


def gram_kernel(scale, wt, act, out):
    feats = act.shape[2]
    for j in range(act.shape[0]):
        tile = jnp.dot(wt[0], act[j], preferred_element_type=jnp.float32) * scale
        out[0, 0, :, j * feats:(j + 1) * feats] = tile


def expanded_mask(block_mask, shard_rows, col_count):
    first_feature = (lax.axis_index("row") * col_count + lax.axis_index("col")) * shard_rows
    block_index = (first_feature + jnp.arange(shard_rows, dtype=jnp.int32)) // BLOCK
    selector = (
        block_index[:, None] == jnp.arange(block_mask.shape[0], dtype=jnp.int32)[None, :]
    ).astype(jnp.float32)
    mask_rows = jnp.dot(selector, block_mask.astype(jnp.float32), precision=lax.Precision.HIGHEST)
    return jnp.repeat(mask_rows, BLOCK, axis=1)


def weigh(activations, token_ids):
    matches = (token_ids[:, None] == token_ids[None, :]).astype(jnp.float32)
    weights = 1.0 / jnp.sum(matches, axis=1)
    return (activations.astype(jnp.float32) * weights[:, None]).astype(jnp.bfloat16)


def kernel_shards(n_row, n_col, activations, token_ids, initial, block_mask):
    rows, feats = activations.shape
    outc = initial.shape[1]
    depth = feats * n_row * n_col
    step_size = rows / (depth + 2.0 * math.sqrt(depth * rows) + rows)
    wt = weigh(activations, token_ids).T
    mask = expanded_mask(block_mask, feats, n_col)
    bf, f32 = jnp.bfloat16, jnp.float32
    small = rows // (n_row * n_col)
    dma = pltpu.SemaphoreType.DMA
    nx = n_col // 2
    any_spec = pl.BlockSpec(memory_space=pl.ANY)
    vmem_spec = pl.BlockSpec(memory_space=pltpu.VMEM)
    wt_cut = wt.reshape(PIECES, feats // PIECES, rows)
    wt_all, act_all, current = pl.pallas_call(
        functools.partial(exchange_kernel, n_row, n_col, step_size),
        out_shape=(
            jax.ShapeDtypeStruct((n_row, PIECES, feats // PIECES, rows), bf),
            jax.ShapeDtypeStruct((n_col, rows, feats), bf),
            jax.ShapeDtypeStruct((feats, outc), f32),
        ),
        in_specs=[any_spec, any_spec] + [vmem_spec] * 4,
        out_specs=(any_spec, any_spec, vmem_spec),
        scratch_shapes=[
            pltpu.VMEM((ITERS, n_col, n_row, small, outc), f32),
            pltpu.VMEM((ITERS, n_col, n_row, small, outc), f32),
            pltpu.VMEM((ITERS, n_row, small, outc), f32),
            pltpu.VMEM((ITERS, n_row, small, outc), f32),
            pltpu.VMEM((ITERS, n_col, n_row, small, outc), f32),
            pltpu.VMEM((feats, 2 * outc), bf),
            pltpu.VMEM((rows, 2 * outc), bf),
            dma((3, n_row, PIECES)), dma((n_row, PIECES)),
            dma((2 * nx,)), dma((n_col,)), dma((2,)),
            dma((ITERS, n_col)), dma((ITERS, n_col)),
            dma((ITERS, n_row)), dma((ITERS, n_row)),
            dma((ITERS, n_row)), dma((ITERS, n_row)),
            dma((ITERS, n_col)), dma((ITERS, n_col)),
        ],
        compiler_params=pltpu.CompilerParams(
            collective_id=0, has_side_effects=True, vmem_limit_bytes=VMEM_LIMIT),
    )(wt_cut, activations, wt, activations, initial, mask)

    tile = feats // PIECES
    wt_tiles = wt_all.reshape(n_row * PIECES, tile, rows)
    gram = pl.pallas_call(
        functools.partial(gram_kernel, 1.0 / rows),
        grid=(n_row * PIECES,),
        out_shape=jax.ShapeDtypeStruct((n_row, 1, feats, n_col * feats), f32),
        in_specs=[
            pl.BlockSpec((1, tile, rows), lambda i: (i, 0, 0)),
            pl.BlockSpec((n_col, rows, feats), lambda i: (0, 0, 0)),
        ],
        out_specs=pl.BlockSpec((1, 1, tile, n_col * feats), lambda i: (i // PIECES, 0, i % PIECES, 0)),
        compiler_params=pltpu.CompilerParams(vmem_limit_bytes=VMEM_LIMIT),
    )(wt_tiles, act_all)
    return gram, current


def shards(n_row, n_col, activations, token_ids, initial, block_mask):
    rows, feats = activations.shape
    if feats % (BLOCK * PIECES) == 0 and n_row % 2 == 0 and n_col % 2 == 0 and rows % (8 * n_row * n_col) == 0:
        return kernel_shards(n_row, n_col, activations, token_ids, initial, block_mask)
    weighted = weigh(activations, token_ids)
    column_panel = lax.all_gather(activations, "col", axis=1, tiled=True)
    gram_tile = lax.dot_general(
        lax.all_gather(weighted, "row", axis=1, tiled=True),
        column_panel,
        (((0,), (0,)), ((), ())),
        preferred_element_type=jnp.float32,
    ) * (1.0 / rows)
    mask_full = expanded_mask(block_mask, feats, n_col)
    depth = feats * n_row * n_col
    step_size = rows / (depth + 2.0 * math.sqrt(depth * rows) + rows)
    current = mask_full * initial
    for iteration in range(ITERS):
        change_now = current - initial
        projected = jnp.dot(
            activations.astype(jnp.float32), change_now, precision=lax.Precision.HIGHEST
        )
        totals = lax.psum(projected, ("row", "col"))
        pulled = lax.dot_general(
            weighted.astype(jnp.float32),
            totals,
            (((0,), (0,)), ((), ())),
            precision=lax.Precision.HIGHEST,
        ) * (1.0 / rows)
        current = mask_full * (current - step_size * pulled)
    return gram_tile.reshape(n_row, 1, feats, gram_tile.shape[1]), current


def solution(mesh):
    in_specs = (
        P("groups", ("row", "col")),
        P("groups"),
        P(("groups", "row", "col"), None),
        P("groups", None),
    )
    out_specs = (P("groups", "col", None, "row"), P(("groups", "row", "col"), None))
    body = functools.partial(shards, mesh.shape["row"], mesh.shape["col"])
    return jax.shard_map(body, mesh=mesh, in_specs=in_specs, out_specs=out_specs, check_vma=False)
```

```python
import functools
import math

import jax
import jax.numpy as jnp
from jax import lax
from jax.experimental import pallas as pl
from jax.experimental.pallas import tpu as pltpu
from jax.sharding import PartitionSpec as P

BLOCK = 128
ITERS = 2
PIECES = 2
TILES = 1
VMEM_LIMIT = 48 * 1024 * 1024


def split_two(value):
    high = value.astype(jnp.bfloat16)
    return high, (value - high.astype(jnp.float32)).astype(jnp.bfloat16)


def exchange_kernel(
    n_row, n_col, step_size,
    wt_hbm, act_hbm, wt, act, init, mask,
    wt_all, act_all, cur,
    partial, from_col, part, from_row, tot, change2, tot2,
    gs, gr, xs, xr, own_sem, s1, r1, s2, r2, s3, r3, s4, r4,
):
    rows = act.shape[0]
    feats, outc = init.shape
    r, c = lax.axis_index("row"), lax.axis_index("col")
    z, y = r // 2, r % 2
    nz = n_row // 2
    x, core = c // 2, c % 2
    nx = n_col // 2
    up, down, side = r + 2, r - 2, z * 2 + (1 - y)
    sibling = x * 2 + (1 - core)
    row_peers = [lax.rem(r + k, n_row) for k in range(1, n_row)]
    col_peers = [lax.rem(c + k, n_col) for k in range(1, n_col)]

    barrier = pltpu.get_barrier_semaphore()
    for p in row_peers:
        pl.semaphore_signal(barrier, inc=1, device_id={"row": p}, device_id_type=pl.DeviceIdType.MESH)
    for p in col_peers:
        pl.semaphore_signal(barrier, inc=1, device_id={"col": p}, device_id_type=pl.DeviceIdType.MESH)
    pl.semaphore_wait(barrier, n_row + n_col - 2)

    def send(src, dst, ss, rs, where):
        return pltpu.make_async_remote_copy(
            src_ref=src, dst_ref=dst, send_sem=ss, recv_sem=rs,
            device_id=where, device_id_type=pl.DeviceIdType.MESH)

    def gcopy(a, h, way, peer, own=False):
        src = wt_hbm.at[h] if own else wt_all.at[a, h]
        return send(src, wt_all.at[a, h], gs.at[way, a, h], gr.at[a, h], {"row": peer})

    def own_pieces(act_on):
        for h in range(PIECES):
            @pl.when(z + 1 < nz)
            def _():
                act_on(gcopy(r, h, 0, up, True))

            @pl.when(z > 0)
            def _():
                act_on(gcopy(r, h, 1, down, True))

            act_on(gcopy(r, h, 2, side, True))

    def hop(d, h, act_on, arrive):
        @pl.when(z >= d)
        def _():
            a = r - 2 * d
            if arrive:
                gcopy(a, h, 2, side).wait_recv()

            @pl.when(z + 1 < nz)
            def _():
                act_on(gcopy(a, h, 0, up))

            act_on(gcopy(a, h, 2, side))

        @pl.when(z + d < nz)
        def _():
            a = r + 2 * d
            if arrive:
                gcopy(a, h, 2, side).wait_recv()

            @pl.when(z > 0)
            def _():
                act_on(gcopy(a, h, 1, down))

            act_on(gcopy(a, h, 2, side))

    start = lambda copy: copy.start()
    wait_send = lambda copy: copy.wait_send()

    hops = [(d, h) for d in range(1, nz) for h in range(PIECES)]
    hops_done = [0]

    def next_hop():
        if hops_done[0] < len(hops):
            d, h = hops[hops_done[0]]
            hop(d, h, start, True)
            hops_done[0] += 1

    def x_copies():
        copies = []
        for k in range(1, nx):
            p = lax.rem(x + k, nx) * 2 + core
            copies.append(send(act_hbm, act_all.at[c], xs.at[k], xr.at[c], {"col": p}))
        copies.append(send(act_hbm, act_all.at[c], xs.at[0], xr.at[c], {"col": sibling}))
        return copies

    def x_passed(k):
        a = lax.rem(x + k, nx) * 2 + core
        return send(act_all.at[a], act_all.at[a], xs.at[nx + k], xr.at[a], {"col": sibling})

    own_wt = pltpu.make_async_copy(wt_hbm, wt_all.at[r], own_sem.at[0])
    own_act = pltpu.make_async_copy(act_hbm, act_all.at[c], own_sem.at[1])
    own_pieces(start)

    chunk = rows // n_col
    cur[...] = mask[...] * init[...]
    pending = []

    for it in range(ITERS):
        high, low = split_two(cur[...] - init[...])
        change2[:, 0:outc] = high
        change2[:, outc:2 * outc] = low

        def project(j, carry):
            a = act[pl.ds(pl.multiple_of(j * chunk, chunk), chunk), :]
            both = jnp.dot(a, change2[...], preferred_element_type=jnp.float32)
            total = both[:, 0:outc] + both[:, outc:2 * outc]
            partial[it, j] = total.reshape(partial.shape[2:])
            return carry

        lax.fori_loop(0, n_col, project, 0)

        def exchange(copies):
            for copy in copies:
                copy.start()
            pending.extend(copies)

        exchange([send(partial.at[it, p], from_col.at[it, c], s1.at[it, k], r1.at[it, c], {"col": p})
                  for k, p in enumerate(col_peers)])
        if it == 0:
            own_wt.start()
            own_act.start()
        next_hop()
        for k, p in enumerate(col_peers):
            send(partial.at[it, p], from_col.at[it, p], s1.at[it, k], r1.at[it, p], {"col": p}).wait_recv()
        acc = partial[it, c]
        for p in col_peers:
            acc = acc + from_col[it, p]
        part[it] = acc
        exchange([send(part.at[it, p], from_row.at[it, r], s2.at[it, k], r2.at[it, r], {"row": p})
                  for k, p in enumerate(row_peers)])
        if it == 0:
            for copy in x_copies():
                copy.start()
        next_hop()
        for k, p in enumerate(row_peers):
            send(part.at[it, p], from_row.at[it, p], s2.at[it, k], r2.at[it, p], {"row": p}).wait_recv()
        acc = part[it, r]
        for p in row_peers:
            acc = acc + from_row[it, p]
        tot[it, c, r] = acc
        exchange([send(tot.at[it, c, r], tot.at[it, c, r], s3.at[it, k], r3.at[it, r], {"row": p})
                  for k, p in enumerate(row_peers)])
        if it > 0:
            next_hop()
        for k, p in enumerate(row_peers):
            send(tot.at[it, c, p], tot.at[it, c, p], s3.at[it, k], r3.at[it, p], {"row": p}).wait_recv()
        exchange([send(tot.at[it, c], tot.at[it, c], s4.at[it, k], r4.at[it, c], {"col": p})
                  for k, p in enumerate(col_peers)])
        next_hop()
        if it == 0:
            for k in range(1, nx):
                a = lax.rem(x + k, nx) * 2 + core
                x_passed(k).wait_recv()
                x_passed(k).start()
        for k, p in enumerate(col_peers):
            send(tot.at[it, p], tot.at[it, p], s4.at[it, k], r4.at[it, p], {"col": p}).wait_recv()

        high, low = split_two(tot[it].reshape(rows, outc))
        tot2[:, 0:outc] = high
        tot2[:, outc:2 * outc] = low

        def pull(j, carry):
            at = pl.ds(pl.multiple_of(j * BLOCK, BLOCK), BLOCK)
            both = jnp.dot(wt[at, :], tot2[...], preferred_element_type=jnp.float32)
            pulled = (both[:, 0:outc] + both[:, outc:2 * outc]) * (1.0 / rows)
            cur[at, :] = mask[at, :] * (cur[at, :] - step_size * pulled)
            return carry

        lax.fori_loop(0, feats // BLOCK, pull, 0)

    while hops_done[0] < len(hops):
        next_hop()
    for zz in range(nz):
        for h in range(PIECES):
            gcopy(zz * 2 + (1 - y), h, 2, side).wait_recv()
    for k in range(nx):
        a = lax.rem(x + k, nx) * 2 + (1 - core)
        send(act_all.at[a], act_all.at[a], xs.at[0], xr.at[a], {"col": sibling}).wait_recv()
    own_pieces(wait_send)
    for d, h in hops:
        hop(d, h, wait_send, False)
    for copy in x_copies():
        copy.wait_send()
    for k in range(1, nx):
        x_passed(k).wait_send()
    for copy in pending:
        copy.wait_send()
    own_wt.wait()
    own_act.wait()


def gram_kernel(scale, wt, act, out):
    feats = act.shape[2]
    for j in range(act.shape[0]):
        tile = jnp.dot(wt[0], act[j], preferred_element_type=jnp.float32) * scale
        out[0, 0, :, j * feats:(j + 1) * feats] = tile


def expanded_mask(block_mask, shard_rows, col_count):
    first_feature = (lax.axis_index("row") * col_count + lax.axis_index("col")) * shard_rows
    block_index = (first_feature + jnp.arange(shard_rows, dtype=jnp.int32)) // BLOCK
    selector = (
        block_index[:, None] == jnp.arange(block_mask.shape[0], dtype=jnp.int32)[None, :]
    ).astype(jnp.float32)
    mask_rows = jnp.dot(selector, block_mask.astype(jnp.float32), precision=lax.Precision.HIGHEST)
    return jnp.repeat(mask_rows, BLOCK, axis=1)


def weigh(activations, token_ids):
    matches = (token_ids[:, None] == token_ids[None, :]).astype(jnp.float32)
    weights = 1.0 / jnp.sum(matches, axis=1)
    return (activations.astype(jnp.float32) * weights[:, None]).astype(jnp.bfloat16)


def kernel_shards(n_row, n_col, activations, token_ids, initial, block_mask):
    rows, feats = activations.shape
    outc = initial.shape[1]
    depth = feats * n_row * n_col
    step_size = rows / (depth + 2.0 * math.sqrt(depth * rows) + rows)
    wt = weigh(activations, token_ids).T
    mask = expanded_mask(block_mask, feats, n_col)
    bf, f32 = jnp.bfloat16, jnp.float32
    small = rows // (n_row * n_col)
    dma = pltpu.SemaphoreType.DMA
    nx = n_col // 2
    any_spec = pl.BlockSpec(memory_space=pl.ANY)
    vmem_spec = pl.BlockSpec(memory_space=pltpu.VMEM)
    wt_cut = wt.reshape(PIECES, feats // PIECES, rows)
    wt_all, act_all, current = pl.pallas_call(
        functools.partial(exchange_kernel, n_row, n_col, step_size),
        out_shape=(
            jax.ShapeDtypeStruct((n_row, PIECES, feats // PIECES, rows), bf),
            jax.ShapeDtypeStruct((n_col, rows, feats), bf),
            jax.ShapeDtypeStruct((feats, outc), f32),
        ),
        in_specs=[any_spec, any_spec] + [vmem_spec] * 4,
        out_specs=(any_spec, any_spec, vmem_spec),
        scratch_shapes=[
            pltpu.VMEM((ITERS, n_col, n_row, small, outc), f32),
            pltpu.VMEM((ITERS, n_col, n_row, small, outc), f32),
            pltpu.VMEM((ITERS, n_row, small, outc), f32),
            pltpu.VMEM((ITERS, n_row, small, outc), f32),
            pltpu.VMEM((ITERS, n_col, n_row, small, outc), f32),
            pltpu.VMEM((feats, 2 * outc), bf),
            pltpu.VMEM((rows, 2 * outc), bf),
            dma((3, n_row, PIECES)), dma((n_row, PIECES)),
            dma((2 * nx,)), dma((n_col,)), dma((2,)),
            dma((ITERS, n_col)), dma((ITERS, n_col)),
            dma((ITERS, n_row)), dma((ITERS, n_row)),
            dma((ITERS, n_row)), dma((ITERS, n_row)),
            dma((ITERS, n_col)), dma((ITERS, n_col)),
        ],
        compiler_params=pltpu.CompilerParams(
            collective_id=0, has_side_effects=True, vmem_limit_bytes=VMEM_LIMIT),
    )(wt_cut, activations, wt, activations, initial, mask)

    tile = feats // TILES
    wt_tiles = wt_all.reshape(n_row * TILES, tile, rows)
    gram = pl.pallas_call(
        functools.partial(gram_kernel, 1.0 / rows),
        grid=(n_row * TILES,),
        out_shape=jax.ShapeDtypeStruct((n_row, 1, feats, n_col * feats), f32),
        in_specs=[
            pl.BlockSpec((1, tile, rows), lambda i: (i, 0, 0)),
            pl.BlockSpec((n_col, rows, feats), lambda i: (0, 0, 0)),
        ],
        out_specs=pl.BlockSpec((1, 1, tile, n_col * feats), lambda i: (i // TILES, 0, i % TILES, 0)),
        compiler_params=pltpu.CompilerParams(vmem_limit_bytes=VMEM_LIMIT),
    )(wt_tiles, act_all)
    return gram, current


def shards(n_row, n_col, activations, token_ids, initial, block_mask):
    rows, feats = activations.shape
    if feats % (BLOCK * PIECES) == 0 and n_row % 2 == 0 and n_col % 2 == 0 and rows % (8 * n_row * n_col) == 0:
        return kernel_shards(n_row, n_col, activations, token_ids, initial, block_mask)
    weighted = weigh(activations, token_ids)
    column_panel = lax.all_gather(activations, "col", axis=1, tiled=True)
    gram_tile = lax.dot_general(
        lax.all_gather(weighted, "row", axis=1, tiled=True),
        column_panel,
        (((0,), (0,)), ((), ())),
        preferred_element_type=jnp.float32,
    ) * (1.0 / rows)
    mask_full = expanded_mask(block_mask, feats, n_col)
    depth = feats * n_row * n_col
    step_size = rows / (depth + 2.0 * math.sqrt(depth * rows) + rows)
    current = mask_full * initial
    for iteration in range(ITERS):
        change_now = current - initial
        projected = jnp.dot(
            activations.astype(jnp.float32), change_now, precision=lax.Precision.HIGHEST
        )
        totals = lax.psum(projected, ("row", "col"))
        pulled = lax.dot_general(
            weighted.astype(jnp.float32),
            totals,
            (((0,), (0,)), ((), ())),
            precision=lax.Precision.HIGHEST,
        ) * (1.0 / rows)
        current = mask_full * (current - step_size * pulled)
    return gram_tile.reshape(n_row, 1, feats, gram_tile.shape[1]), current


def solution(mesh):
    in_specs = (
        P("groups", ("row", "col")),
        P("groups"),
        P(("groups", "row", "col"), None),
        P("groups", None),
    )
    out_specs = (P("groups", "col", None, "row"), P(("groups", "row", "col"), None))
    body = functools.partial(shards, mesh.shape["row"], mesh.shape["col"])
    return jax.shard_map(body, mesh=mesh, in_specs=in_specs, out_specs=out_specs, check_vma=False)
```
